128 devices in a mesh: outer: 4 (over y_lo, core), blk: 32 (over z, x, y_hi).
Axes of the slice: x: 4, y: 4 (y_hi: 2, y_lo: 2; y = y_hi * 2 + y_lo), z: 4, core: 2. Of those that a mesh axis runs over, the one named last changes fastest.
Arguments:
- images: bfloat16 [81920, 1152], P(('outer', 'blk')), may hold values from -0.1796875 to 0.1796875
- texts: bfloat16 [81920, 1152], P(('outer', 'blk')), may hold values from -0.1796875 to 0.1796875
- log_scale: float32 [1], replicated, may hold values from 1.5 to 2.5
- bias: float32 [1], replicated, may hold values from -4 to -1
Outputs:
- row_loss: float32 [81920], P(('outer', 'blk'))
- image_grad: float32 [81920, 1152], P(('outer', 'blk'))
- text_grad: float32 [81920, 1152], P(('outer', 'blk'))
The draws below stay inside these ranges and needn't reach their ends.
All inputs are finite; a program needn't handle non-finite values.
Results may differ from the reference program's by a relative error of at most 0.0044.
Values may be sent and summed in bfloat16 or wider, within the bound.
No kernel may reach another device: no remote copies, remote signals or barrier semaphores. Data moves between devices by JAX's collectives and lax.ppermute only.
A program may use at most 128 MiB of HBM per device.

```python
import jax
import jax.numpy as jnp
from jax import lax

D = 1152
ROWS = 640
STEPS = 4
TOTAL = 81920
N_OUTER = 4
N_BLK = 32


def block_levels(own_key, dims, pieces, smallest, largest):
    factor_of = 1.0
    for position, parts in pieces:
        steps = jax.random.uniform(jax.random.fold_in(jax.random.fold_in(own_key, 6), position), (parts,), jnp.float32, smallest / len(pieces), largest / len(pieces))
        factor_of = factor_of * jnp.repeat(jnp.exp(steps), dims[position] // parts).reshape((-1,) + (1,) * (len(dims) - 1 - position))
    return factor_of


def normal_values(stream_key, dims, width, most, cuts=(), held_as=jnp.bfloat16):
    result = jax.random.normal(stream_key, dims, jnp.float32) * width
    if len(cuts) > 0:
        result = block_levels(stream_key, dims, cuts, -0.22, 0.18) * result
    return jnp.clip(result, min=-most, max=most).astype(held_as)


def setup_inputs(seed: int = 0) -> dict:
    seeds = jax.random.split(jax.random.key(seed), 5)
    images = normal_values(seeds[0], (TOTAL, D), 0.03, 0.1796875, ((0, 128),))
    texts = normal_values(seeds[1], (TOTAL, D), 0.03, 0.1796875, ((0, 128),))
    log_scale = jnp.clip(jax.random.uniform(seeds[2], (1,), jnp.float32, 1.5, 2.5), 1.5, 2.5)
    bias = jnp.clip(jax.random.uniform(seeds[3], (1,), jnp.float32, -4.0, -1.0), -4.0, -1.0)
    return dict(images=images, texts=texts, log_scale=log_scale, bias=bias)


def unit_rows(raw):
    wide = raw.astype(jnp.float32)
    inverse = lax.rsqrt(lax.optimization_barrier(jnp.sum(wide * wide, axis=-1, keepdims=True)) + 1e-06)
    return (wide * inverse, inverse)

def reference(images, texts, log_scale, bias):
    unit_img, inv_img = unit_rows(images)
    unit_txt, inv_txt = unit_rows(texts)
    shape = (N_OUTER, N_BLK, ROWS, images.shape[1])
    img_low = unit_img.astype(jnp.bfloat16).astype(jnp.float32).reshape(shape)
    txt_low = unit_txt.astype(jnp.bfloat16).astype(jnp.float32).reshape(shape)
    scale = jnp.exp(log_scale[0])
    offset = bias[0]
    eye = jnp.eye(ROWS, dtype=jnp.bool_)
    unit_grad = jnp.zeros(shape, jnp.float32)
    txt_grad = jnp.zeros(shape, jnp.float32)
    row_sum = jnp.zeros(shape[:3], jnp.float32)
    shifts = [(0, k) for k in range(STEPS + 1)] + [(1, 0)]
    for group_shift, block_shift in shifts:
        visit = jnp.roll(txt_low, (group_shift, block_shift), axis=(0, 1))
        logits = scale * jnp.einsum('onrd,onsd->onrs', img_low, visit) + offset
        if group_shift == 0 and block_shift == 0:
            sign = jnp.where(eye, jnp.float32(1.0), jnp.float32(-1.0))
        else:
            sign = jnp.float32(-1.0)
        row_sum = row_sum + lax.optimization_barrier(jnp.sum(jax.nn.softplus(-sign * logits), axis=-1))
        slope = (scale * -sign * jax.nn.sigmoid(-sign * logits)).astype(jnp.bfloat16).astype(jnp.float32)
        unit_grad = unit_grad + jnp.einsum('onrs,onsd->onrd', slope, visit)
        part = jnp.einsum('onrs,onrd->onsd', slope, img_low)
        txt_grad = txt_grad + jnp.roll(part, (-group_shift, -block_shift), axis=(0, 1))
    unit_grad = unit_grad.reshape(images.shape)
    txt_grad = txt_grad.reshape(texts.shape)
    image_grad = (unit_grad - unit_img * lax.optimization_barrier(jnp.sum(unit_img * unit_grad, axis=1, keepdims=True))) * inv_img
    text_grad = (txt_grad - unit_txt * lax.optimization_barrier(jnp.sum(unit_txt * txt_grad, axis=1, keepdims=True))) * inv_txt
    row_loss = row_sum.reshape(-1) / jnp.float32((STEPS + 2) * ROWS)
    return (row_loss, image_grad, text_grad)
```

```python
import functools

import jax
import jax.numpy as jnp
from jax import lax
from jax.experimental import pallas as pl
from jax.experimental.pallas import tpu as pltpu
from jax.sharding import PartitionSpec as P

STEPS = 4
LOG2E = 1.4426950408889634
LN2 = 0.6931471805599453
VMEM_LIMIT = 48 * 1024 * 1024


def normalize_kernel(odd_ref, img_ref, txt_ref, a_ref, b_ref):
    img = img_ref[...].astype(jnp.float32)
    txt = txt_ref[...].astype(jnp.float32)
    img = img * lax.rsqrt(jnp.sum(img * img, axis=-1, keepdims=True) + 1e-06)
    txt = txt * lax.rsqrt(jnp.sum(txt * txt, axis=-1, keepdims=True) + 1e-06)
    odd = odd_ref[0] == 1
    a_ref[...] = jnp.where(odd, txt, img).astype(jnp.bfloat16)
    b_ref[...] = jnp.where(odd, img, txt).astype(jnp.bfloat16)


def normalize(odd, images, texts):
    rows, width = images.shape
    tile = rows // 4
    spec = pl.BlockSpec((tile, width), lambda i: (i, 0))
    return pl.pallas_call(
        normalize_kernel,
        grid=(rows // tile,),
        in_specs=[pl.BlockSpec(memory_space=pltpu.SMEM), spec, spec],
        out_specs=[spec, spec],
        out_shape=[jax.ShapeDtypeStruct(images.shape, jnp.bfloat16)] * 2,
        compiler_params=pltpu.CompilerParams(vmem_limit_bytes=VMEM_LIMIT),
    )(odd, images, texts)


def lane_sums(x):
    total = x[:, 0:128]
    for start in range(128, x.shape[1], 128):
        total = total + x[:, start : start + 128]
    return total


def visit_kernel(first, coef_ref, own_ref, other_ref, *refs):
    if first:
        acc_ref, loss_ref = refs
    else:
        acc_in, loss_in, acc_ref, loss_ref = refs
    scale = coef_ref[0]
    own = own_ref[...]
    other = other_ref[...]
    dots = lax.dot_general(
        own, other, (((1,), (1,)), ((), ())), preferred_element_type=jnp.float32
    )
    z2 = dots * coef_ref[1] + coef_ref[2]
    e = jnp.exp2(z2)
    u = 1.0 + e
    r = 1.0 / u
    loss = jnp.log2(u) * LN2 + (e - (u - 1.0)) * r
    slope = scale * (e * r)
    if first:
        tile = own.shape[0]
        rows = lax.broadcasted_iota(jnp.int32, dots.shape, 0) + pl.program_id(0) * tile
        cols = lax.broadcasted_iota(jnp.int32, dots.shape, 1)
        match = rows == cols
        loss = jnp.where(match, loss - z2 * LN2, loss)
        slope = jnp.where(match, -scale * r, slope)
    part = jnp.dot(slope.astype(jnp.bfloat16), other, preferred_element_type=jnp.float32)
    sums = lane_sums(loss)
    if first:
        acc_ref[...] = part
        loss_ref[...] = sums
    else:
        acc_ref[...] = acc_in[...] + part
        loss_ref[...] = loss_in[...] + sums


def visit(coef, own, other, acc=None, tile=320):
    rows, width = own.shape
    first = acc is None
    own_spec = pl.BlockSpec((tile, width), lambda i: (i, 0))
    all_spec = pl.BlockSpec((rows, width), lambda i: (0, 0))
    loss_spec = pl.BlockSpec((tile, 128), lambda i: (i, 0))
    accs = () if first else tuple(acc)
    return pl.pallas_call(
        functools.partial(visit_kernel, first),
        grid=(rows // tile,),
        in_specs=[pl.BlockSpec(memory_space=pltpu.SMEM), own_spec, all_spec]
        + ([] if first else [own_spec, loss_spec]),
        out_specs=[own_spec, loss_spec],
        out_shape=[
            jax.ShapeDtypeStruct((rows, width), jnp.float32),
            jax.ShapeDtypeStruct((rows, 128), jnp.float32),
        ],
        input_output_aliases={} if first else {3: 0, 4: 1},
        cost_estimate=pl.CostEstimate(
            flops=4 * rows * rows * width,
            bytes_accessed=12 * rows * width,
            transcendentals=3 * rows * rows,
        ),
        compiler_params=pltpu.CompilerParams(vmem_limit_bytes=VMEM_LIMIT),
    )(coef, own, other, *accs)


def project(raw, grad):
    wide = raw.astype(jnp.float32)
    inverse = lax.rsqrt(jnp.sum(wide * wide, axis=-1, keepdims=True) + 1e-06)
    unit = wide * inverse
    return (grad - unit * jnp.sum(unit * grad, axis=1, keepdims=True)) * inverse


def finish_kernel(odd_ref, img_ref, txt_ref, acc_a, acc_b, img_out, txt_out):
    odd = odd_ref[0] == 1
    a, b = acc_a[...], acc_b[...]
    img_out[...] = project(img_ref[...], jnp.where(odd, b, a))
    txt_out[...] = project(txt_ref[...], jnp.where(odd, a, b))


def finish(odd, images, texts, acc_a, acc_b):
    rows, width = images.shape
    tile = rows // 4
    spec = pl.BlockSpec((tile, width), lambda i: (i, 0))
    return pl.pallas_call(
        finish_kernel,
        grid=(rows // tile,),
        in_specs=[pl.BlockSpec(memory_space=pltpu.SMEM)] + [spec] * 4,
        out_specs=[spec, spec],
        out_shape=[jax.ShapeDtypeStruct(images.shape, jnp.float32)] * 2,
        compiler_params=pltpu.CompilerParams(vmem_limit_bytes=VMEM_LIMIT),
    )(odd, images, texts, acc_a, acc_b)


def body(images, texts, log_scale, bias):
    groups, places = lax.axis_size("outer"), lax.axis_size("blk")
    both = ("outer", "blk")

    def along(x, odd_by, even_by):
        pairs = [(i, (i + (odd_by if i % 2 else even_by)) % places) for i in range(places)]
        return lax.ppermute(x, "blk", pairs)

    def across(x, odd_by, even_by):
        pairs = []
        for o in range(groups):
            for c in range(places):
                to = (o + (odd_by if c % 2 else even_by)) % groups
                pairs.append((o * places + c, to * places + c))
        return lax.ppermute(x, both, pairs)

    odd = (lax.axis_index("blk") % 2).astype(jnp.int32).reshape(1)
    scale = jnp.exp(log_scale[0])
    coef = jnp.stack([scale, scale * LOG2E, bias[0] * LOG2E])

    a, b = normalize(odd, images, texts)
    a1 = along(a, 2, -2)
    b1 = along(b, -2, 2)
    u = along(b, -1, 1)
    of_a = visit(coef, a, b)
    of_b = visit(coef, b, a)
    a1, b1, u, of_a, of_b = lax.optimization_barrier((a1, b1, u, of_a, of_b))
    v = along(a1, -1, 1)
    a2 = along(a1, 2, -2)
    b2 = along(b1, -2, 2)
    of_b = visit(coef, b, a1, of_b)
    of_a = visit(coef, a, b1, of_a)
    of_b = visit(coef, b, u, of_b)
    u, a, b, v, of_a, of_b = lax.optimization_barrier((u, a, b, v, of_a, of_b))
    w2 = along(v, -2, 2)
    w1 = along(u, 2, -2)
    a_out = across(a, 1, -1)
    b_out = across(b, -1, 1)
    of_a = visit(coef, a, v, of_a)
    of_b = visit(coef, b, a2, of_b)
    of_a = visit(coef, a, b2, of_a)
    of_b = visit(coef, b, a_out, of_b)
    of_a = visit(coef, a, b_out, of_a)
    of_b = visit(coef, b, w1, of_b)
    of_a = visit(coef, a, w2, of_a)
    image_grad, text_grad = finish(odd, images, texts, of_a[0], of_b[0])
    losses = jnp.where(odd[0] == 1, of_b[1], of_a[1])
    row_loss = jnp.sum(losses, axis=1) / jnp.float32((STEPS + 2) * images.shape[0])
    return (row_loss, image_grad, text_grad)


def solution(mesh):
    return jax.shard_map(
        body,
        mesh=mesh,
        in_specs=(P(("outer", "blk"), None), P(("outer", "blk"), None), P(), P()),
        out_specs=(P(("outer", "blk")), P(("outer", "blk"), None), P(("outer", "blk"), None)),
        check_vma=False,
    )
```

```python
import functools

import jax
import jax.numpy as jnp
from jax import lax
from jax.experimental import pallas as pl
from jax.experimental.pallas import tpu as pltpu
from jax.sharding import PartitionSpec as P

STEPS = 4
LOG2E = 1.4426950408889634
LN2 = 0.6931471805599453
UPPER = 384
VMEM_LIMIT = 28 * 1024 * 1024
COST = 1000
SPLIT = 1


def normalize_kernel(odd_ref, img_hbm, txt_hbm, a_hbm, b_hbm, raw, out, sems):
    rows = img_hbm.shape[0]
    tile = 128
    odd = odd_ref[0] == 1
    loads, stores = [], []
    for k, start in enumerate(range(0, rows, tile)):
        here = pl.ds(start, tile)
        for j, ref in enumerate((img_hbm, txt_hbm)):
            loads.append(pltpu.make_async_copy(ref.at[here], raw.at[j, here], sems.at[2 * k + j]))
            loads[-1].start()
    used = len(loads)
    for k, start in enumerate(range(0, rows, tile)):
        here = pl.ds(start, tile)
        units = []
        for j in range(2):
            loads[2 * k + j].wait()
            wide = raw[j, start : start + tile, :].astype(jnp.float32)
            inverse = lax.rsqrt(jnp.sum(wide * wide, axis=-1, keepdims=True) + 1e-06)
            units.append((wide * inverse).astype(jnp.bfloat16))
        out[0, start : start + tile, :] = jnp.where(odd, units[1], units[0])
        out[1, start : start + tile, :] = jnp.where(odd, units[0], units[1])
        for role, ref in ((0, a_hbm), (1, b_hbm)):
            stores.append(pltpu.make_async_copy(out.at[role, here], ref.at[here], sems.at[used]))
            stores[-1].start()
            used += 1
    for store in stores:
        store.wait()


def normalize(odd, images, texts):
    rows, width = images.shape
    hbm = pl.BlockSpec(memory_space=pl.ANY)
    return pl.pallas_call(
        normalize_kernel,
        in_specs=[pl.BlockSpec(memory_space=pltpu.SMEM), hbm, hbm],
        out_specs=[hbm] * 2,
        out_shape=[jax.ShapeDtypeStruct((rows, width), jnp.bfloat16)] * 2,
        scratch_shapes=[
            pltpu.VMEM((2, rows, width), jnp.bfloat16),
            pltpu.VMEM((2, rows, width), jnp.bfloat16),
            pltpu.SemaphoreType.DMA((4 * rows // 128,)),
        ],
        compiler_params=pltpu.CompilerParams(vmem_limit_bytes=60 * 1024 * 1024),
    )(odd, images, texts)


def lane_sums(x):
    total = x[:, 0:128]
    for start in range(128, x.shape[1], 128):
        total = total + x[:, start : start + 128]
    return total


def project(raw, grad):
    wide = raw.astype(jnp.float32)
    inverse = lax.rsqrt(jnp.sum(wide * wide, axis=-1, keepdims=True) + 1e-06)
    unit = wide * inverse
    return (grad - unit * jnp.sum(unit * grad, axis=1, keepdims=True)) * inverse


def group_kernel(plan, emit, first, last, tile, odd_ref, coef_ref, *refs):
    count = sum(n for _, n in plan)
    refs = list(refs)
    take = lambda n: [refs.pop(0) for _ in range(n)]
    own_hbm = take(2)
    visits = [] if first else take(count)
    acc_hbm, loss_hbm = (None, None) if first else take(2)
    raw_hbm = take(2) if last else None
    outs = take(3 if last else 2)
    emitted = take(len(emit))
    own, other, acc, loss, sems = take(5)
    raw = take(1)[0] if last else None
    rows = own.shape[1]
    scale = coef_ref[0]
    odd = odd_ref[0] == 1
    used = [0]

    def copy(src, dst, src_at=0, dst_at=0, n=None):
        step = n // SPLIT
        each = []
        for k in range(SPLIT):
            used[0] += 1
            each.append(
                pltpu.make_async_copy(
                    src.at[pl.ds(src_at + k * step, step)],
                    dst.at[pl.ds(dst_at + k * step, step)],
                    sems.at[used[0] - 1],
                )
            )
        return each

    def start_all(each):
        for one in each:
            one.start()

    def wait_all(each):
        for one in each:
            one.wait()

    own_in, acc_in, raw_in, visit_in = {}, {}, {}, []
    starts = [0]
    for ref in visits:
        starts.append(starts[-1] + ref.shape[0])
    for role, n in plan:
        if role not in own_in:
            own_in[role] = copy(own_hbm[role], own.at[role], n=rows)
            start_all(own_in[role])
        for _ in range(0 if first else n):
            k = len(visit_in)
            visit_in.append(copy(visits[k], other, dst_at=starts[k], n=visits[k].shape[0]))
            start_all(visit_in[k])
        if not first and role not in acc_in:
            acc_in[role] = copy(acc_hbm.at[role], acc.at[role], n=rows)
            acc_in[role] += copy(loss_hbm.at[role], loss.at[role], n=rows)
            start_all(acc_in[role])
        if last and role not in raw_in:
            used[0] += 1
            sem = sems.at[used[0] - 1]
            straight = pltpu.make_async_copy(raw_hbm[0], raw.at[role], sem)
            crossed = pltpu.make_async_copy(raw_hbm[1], raw.at[role], sem)
            from_img = odd if role == 1 else jnp.logical_not(odd)
            pl.when(from_img)(straight.start)
            pl.when(jnp.logical_not(from_img))(crossed.start)
            raw_in[role] = straight

    stores = []
    done = 0
    for index, (role, n) in enumerate(plan):
        final = role not in [r for r, _ in plan[index + 1 :]]
        opening = role not in [r for r, _ in plan[:index]]
        if opening and not (first and index):
            wait_all(own_in[role] + (own_in[1 - role] if first else []))
        for k in range(done, 0 if first else done + n):
            wait_all(visit_in[k])
        for (k, at, n_rows), ref in zip(emit, emitted):
            if done <= k < done + n:
                each = copy(other, ref, src_at=starts[k] + at, n=n_rows)
                start_all(each)
                stores += each
        for start in range(0, rows, tile):
            part_rows = slice(start, start + tile)
            mine = own[role, part_rows, :]
            theirs = own[1 - role] if first else other[starts[done] : starts[done + n], :]
            dots = lax.dot_general(
                mine, theirs, (((1,), (1,)), ((), ())), preferred_element_type=jnp.float32
            )
            z2 = dots * coef_ref[1] + coef_ref[2]
            e = jnp.exp2(z2)
            u = 1.0 + e
            r = 1.0 / u
            losses = jnp.log2(u) * LN2 + (e - (u - 1.0)) * r
            slope = scale * (e * r)
            if first:
                at = lax.broadcasted_iota(jnp.int32, dots.shape, 0) + start
                match = at == lax.broadcasted_iota(jnp.int32, dots.shape, 1)
                losses = jnp.where(match, losses - z2 * LN2, losses)
                slope = jnp.where(match, -scale * r, slope)
            grad = jnp.dot(slope.astype(jnp.bfloat16), theirs, preferred_element_type=jnp.float32)
            sums = lane_sums(losses)
            if opening and not first:
                if start == 0:
                    wait_all(acc_in[role])
            if not (first and opening):
                grad = acc[role, part_rows, :] + grad
                sums = loss[role, part_rows, :] + sums
            loss[role, part_rows, :] = sums
            if last and final:
                if start == 0:
                    raw_in[role].wait()
                grad = project(raw[role, part_rows, :], grad)
            acc[role, part_rows, :] = grad
            if final and last:
                used[0] += 1
                sem = sems.at[used[0] - 1]
                piece = acc.at[role, pl.ds(start, tile)]
                straight = pltpu.make_async_copy(piece, outs[0].at[pl.ds(start, tile)], sem)
                crossed = pltpu.make_async_copy(piece, outs[1].at[pl.ds(start, tile)], sem)
                to_img = odd if role == 1 else jnp.logical_not(odd)
                pl.when(to_img)(straight.start)
                pl.when(jnp.logical_not(to_img))(crossed.start)
                stores.append(straight)
        if final and not last:
            for ref, out in ((acc, outs[0]), (loss, outs[1])):
                each = copy(ref.at[role], out.at[role], n=rows)
                start_all(each)
                stores += each
        done += n
    if last:
        picked = jnp.where(odd, loss[1], loss[0])
        for k in range(rows // 128):
            block = jnp.transpose(picked[k * 128 : (k + 1) * 128, :])
            outs[2][k : k + 1, :] = jnp.sum(block, axis=0, keepdims=True) / jnp.float32((STEPS + 2) * rows)
    for store in stores:
        store.wait()


def group(odd, coef, own, plan, visits, state=None, raws=None, emit=(), tile=320):
    rows, width = own[0].shape
    first, last = state is None, raws is not None
    count = sum(n for _, n in plan)
    met = sum(x.shape[0] for x in visits)
    hbm, smem = pl.BlockSpec(memory_space=pl.ANY), pl.BlockSpec(memory_space=pltpu.SMEM)
    args = [*own, *visits, *(state or ()), *(raws or ())]
    f32 = jnp.float32
    if last:
        out_shape = [jax.ShapeDtypeStruct((rows, width), f32)] * 2 + [
            jax.ShapeDtypeStruct((rows // 128, 128), f32)
        ]
        out_specs = [hbm, hbm, pl.BlockSpec(memory_space=pltpu.VMEM)]
    else:
        out_shape = [
            jax.ShapeDtypeStruct((2, rows, width), f32),
            jax.ShapeDtypeStruct((2, rows, 128), f32),
        ]
        out_shape += [jax.ShapeDtypeStruct((n, width), jnp.bfloat16) for _, _, n in emit]
        out_specs = [hbm] * len(out_shape)
    scratch = [
        pltpu.VMEM((2, rows, width), jnp.bfloat16),
        pltpu.VMEM((max(met, 16), width), jnp.bfloat16),
        pltpu.VMEM((2, rows, width), f32),
        pltpu.VMEM((2, rows, 128), f32),
        pltpu.SemaphoreType.DMA((96,)),
    ]
    if last:
        scratch.append(pltpu.VMEM((2, rows, width), jnp.bfloat16))
    return pl.pallas_call(
        functools.partial(group_kernel, plan, emit, first, last, tile),
        in_specs=[smem, smem] + [hbm] * len(args),
        out_specs=out_specs,
        out_shape=out_shape,
        scratch_shapes=scratch,
        input_output_aliases={} if first or last else {4 + count: 0, 5 + count: 1},
        cost_estimate=pl.CostEstimate(flops=COST, bytes_accessed=COST, transcendentals=0),
        compiler_params=pltpu.CompilerParams(vmem_limit_bytes=VMEM_LIMIT),
    )(odd, coef, *args)


def body(images, texts, log_scale, bias):
    groups, places = lax.axis_size("outer"), lax.axis_size("blk")
    both = ("outer", "blk")

    def along(x, odd_by, even_by):
        pairs = [(i, (i + (odd_by if i % 2 else even_by)) % places) for i in range(places)]
        return lax.ppermute(x, "blk", pairs)

    def across(x, odd_by, even_by):
        pairs = []
        for o in range(groups):
            for c in range(places):
                to = (o + (odd_by if c % 2 else even_by)) % groups
                pairs.append((o * places + c, to * places + c))
        return lax.ppermute(x, both, pairs)

    odd = (lax.axis_index("blk") % 2).astype(jnp.int32).reshape(1)
    scale = jnp.exp(log_scale[0])
    coef = jnp.stack([scale, scale * LOG2E, bias[0] * LOG2E])

    gate = lax.optimization_barrier
    a, b = own = normalize(odd, images, texts)
    a1 = along(a, 2, -2)
    u = along(b, -1, 1)
    b1 = along(b, -2, 2)
    state = group(odd, coef, own, ((0, 1), (1, 1)), ())
    a1, state = gate((a1, state))
    v = along(a1, -1, 1)
    a2 = along(a1, 2, -2)
    b1, u, state = gate((b1, u, state))
    b2 = along(b1, -2, 2)
    *state, ux, uy = group(
        odd, coef, own, ((1, 2), (0, 1)), (a1, u, b1), state,
        emit=((1, 0, UPPER), (1, UPPER, a.shape[0] - UPPER)),
    )
    ux, uy, v, a, b, state = gate((ux, uy, v, a, b, state))
    w2 = along(v, -2, 2)
    w1x = along(ux, 2, -2)
    w1y = along(uy, 2, -2)
    a_out = across(a, 1, -1)
    b_out = across(b, -1, 1)
    state = group(odd, coef, own, ((0, 2), (1, 1)), (v, b2, a2), state)
    state = group(odd, coef, own, ((1, 2),), (a_out, w1x), state)
    image_grad, text_grad, row_loss = group(
        odd, coef, own, ((1, 1), (0, 2)), (w1y, b_out, w2), state, (images, texts)
    )
    row_loss = row_loss.reshape(images.shape[0])
    return (row_loss, image_grad, text_grad)


def solution(mesh):
    return jax.shard_map(
        body,
        mesh=mesh,
        in_specs=(P(("outer", "blk"), None), P(("outer", "blk"), None), P(), P()),
        out_specs=(P(("outer", "blk")), P(("outer", "blk"), None), P(("outer", "blk"), None)),
        check_vma=False,
    )
```

```python
import functools

import jax
import jax.numpy as jnp
from jax import lax
from jax.experimental import pallas as pl
from jax.experimental.pallas import tpu as pltpu
from jax.sharding import PartitionSpec as P

STEPS = 4
LOG2E = 1.4426950408889634
LN2 = 0.6931471805599453
UPPER = 384
VMEM_LIMIT = 28 * 1024 * 1024
COST = 1000


def normalize_kernel(odd_ref, img_hbm, txt_hbm, a_hbm, b_hbm, raw, out, sems):
    rows = img_hbm.shape[0]
    tile = 128
    odd = odd_ref[0] == 1
    loads, stores = [], []
    for k, start in enumerate(range(0, rows, tile)):
        here = pl.ds(start, tile)
        for j, ref in enumerate((img_hbm, txt_hbm)):
            loads.append(pltpu.make_async_copy(ref.at[here], raw.at[j, here], sems.at[2 * k + j]))
            loads[-1].start()
    used = len(loads)
    for k, start in enumerate(range(0, rows, tile)):
        here = pl.ds(start, tile)
        units = []
        for j in range(2):
            loads[2 * k + j].wait()
            wide = raw[j, start : start + tile, :].astype(jnp.float32)
            inverse = lax.rsqrt(jnp.sum(wide * wide, axis=-1, keepdims=True) + 1e-06)
            units.append((wide * inverse).astype(jnp.bfloat16))
        out[0, start : start + tile, :] = jnp.where(odd, units[1], units[0])
        out[1, start : start + tile, :] = jnp.where(odd, units[0], units[1])
        for role, ref in ((0, a_hbm), (1, b_hbm)):
            stores.append(pltpu.make_async_copy(out.at[role, here], ref.at[here], sems.at[used]))
            stores[-1].start()
            used += 1
    for store in stores:
        store.wait()


def normalize(odd, images, texts):
    rows, width = images.shape
    hbm = pl.BlockSpec(memory_space=pl.ANY)
    return pl.pallas_call(
        normalize_kernel,
        in_specs=[pl.BlockSpec(memory_space=pltpu.SMEM), hbm, hbm],
        out_specs=[hbm] * 2,
        out_shape=[jax.ShapeDtypeStruct((rows, width), jnp.bfloat16)] * 2,
        scratch_shapes=[
            pltpu.VMEM((2, rows, width), jnp.bfloat16),
            pltpu.VMEM((2, rows, width), jnp.bfloat16),
            pltpu.SemaphoreType.DMA((4 * rows // 128,)),
        ],
        compiler_params=pltpu.CompilerParams(vmem_limit_bytes=60 * 1024 * 1024),
    )(odd, images, texts)


def lane_sums(x):
    total = x[:, 0:128]
    for start in range(128, x.shape[1], 128):
        total = total + x[:, start : start + 128]
    return total


def project(raw, grad):
    wide = raw.astype(jnp.float32)
    inverse = lax.rsqrt(jnp.sum(wide * wide, axis=-1, keepdims=True) + 1e-06)
    unit = wide * inverse
    return (grad - unit * jnp.sum(unit * grad, axis=1, keepdims=True)) * inverse


def group_kernel(plan, emit, first, last, tile, odd_ref, coef_ref, *refs):
    count = sum(n for _, n in plan)
    refs = list(refs)
    take = lambda n: [refs.pop(0) for _ in range(n)]
    own = take(2)
    visits = [] if first else take(count)
    acc_in, loss_in = (None, None) if first else take(2)
    raws = take(2) if last else None
    outs = take(3 if last else 2)
    emitted = take(len(emit))
    acc, loss = take(2) if last else outs
    sems = take(1)[0] if last else None
    rows = own[0].shape[0]
    scale = coef_ref[0]
    odd = odd_ref[0] == 1
    for (k, at, n), ref in zip(emit, emitted):
        ref[...] = visits[k][at : at + n, :]
    stores = []
    done = 0
    for index, (role, n) in enumerate(plan):
        final = role not in [r for r, _ in plan[index + 1 :]]
        opening = role not in [r for r, _ in plan[:index]]
        others = [own[1 - role]] if first else visits[done : done + n]
        theirs = jnp.concatenate([ref[...] for ref in others], axis=0)
        for start in range(0, rows, tile):
            part_rows = slice(start, start + tile)
            dots = lax.dot_general(
                own[role][part_rows, :],
                theirs,
                (((1,), (1,)), ((), ())),
                preferred_element_type=jnp.float32,
            )
            z2 = dots * coef_ref[1] + coef_ref[2]
            e = jnp.exp2(z2)
            u = 1.0 + e
            r = 1.0 / u
            losses = jnp.log2(u) * LN2 + (e - (u - 1.0)) * r
            slope = scale * (e * r)
            if first:
                at = lax.broadcasted_iota(jnp.int32, dots.shape, 0) + start
                match = at == lax.broadcasted_iota(jnp.int32, dots.shape, 1)
                losses = jnp.where(match, losses - z2 * LN2, losses)
                slope = jnp.where(match, -scale * r, slope)
            grad = jnp.dot(slope.astype(jnp.bfloat16), theirs, preferred_element_type=jnp.float32)
            sums = lane_sums(losses)
            if not (first and opening):
                held, held_loss = (acc_in, loss_in) if opening else (acc, loss)
                grad = held[role, part_rows, :] + grad
                sums = held_loss[role, part_rows, :] + sums
            loss[role, part_rows, :] = sums
            if not (last and final):
                acc[role, part_rows, :] = grad
                continue
            is_img = odd if role == 1 else jnp.logical_not(odd)
            raw = jnp.where(is_img, raws[0][part_rows, :], raws[1][part_rows, :])
            acc[role, part_rows, :] = project(raw, grad)
            sem = sems.at[len(stores)]
            piece = acc.at[role, pl.ds(start, tile)]
            to_img = pltpu.make_async_copy(piece, outs[0].at[pl.ds(start, tile)], sem)
            to_txt = pltpu.make_async_copy(piece, outs[1].at[pl.ds(start, tile)], sem)
            pl.when(is_img)(to_img.start)
            pl.when(jnp.logical_not(is_img))(to_txt.start)
            stores.append(to_img)
        done += n
    if last:
        picked = jnp.where(odd, loss[1], loss[0])
        for k in range(rows // 128):
            block = jnp.transpose(picked[k * 128 : (k + 1) * 128, :])
            outs[2][k : k + 1, :] = jnp.sum(block, axis=0, keepdims=True) / jnp.float32((STEPS + 2) * rows)
    for store in stores:
        store.wait()


def group(odd, coef, own, plan, visits, state=None, raws=None, emit=(), tile=320):
    rows, width = own[0].shape
    first, last = state is None, raws is not None
    count = sum(n for _, n in plan)
    vmem, smem = pl.BlockSpec(memory_space=pltpu.VMEM), pl.BlockSpec(memory_space=pltpu.SMEM)
    args = [*own, *visits, *(state or ()), *(raws or ())]
    f32 = jnp.float32
    sums = [(2, rows, width), (2, rows, 128)]
    scratch = []
    if last:
        hbm = pl.BlockSpec(memory_space=pl.ANY)
        out_shape = [jax.ShapeDtypeStruct((rows, width), f32)] * 2 + [
            jax.ShapeDtypeStruct((rows // 128, 128), f32)
        ]
        out_specs = [hbm, hbm, vmem]
        scratch = [pltpu.VMEM(shape, f32) for shape in sums]
        scratch.append(pltpu.SemaphoreType.DMA((2 * rows // tile,)))
    else:
        out_shape = [jax.ShapeDtypeStruct(shape, f32) for shape in sums]
        out_shape += [jax.ShapeDtypeStruct((n, width), jnp.bfloat16) for _, _, n in emit]
        out_specs = [vmem] * len(out_shape)
    return pl.pallas_call(
        functools.partial(group_kernel, plan, emit, first, last, tile),
        in_specs=[smem, smem] + [vmem] * len(args),
        out_specs=out_specs,
        out_shape=out_shape,
        scratch_shapes=scratch,
        input_output_aliases={} if first or last else {4 + count: 0, 5 + count: 1},
        cost_estimate=pl.CostEstimate(flops=COST, bytes_accessed=COST, transcendentals=0),
        compiler_params=pltpu.CompilerParams(vmem_limit_bytes=VMEM_LIMIT),
    )(odd, coef, *args)


def body(images, texts, log_scale, bias):
    groups, places = lax.axis_size("outer"), lax.axis_size("blk")
    both = ("outer", "blk")

    def along(x, odd_by, even_by):
        pairs = [(i, (i + (odd_by if i % 2 else even_by)) % places) for i in range(places)]
        return lax.ppermute(x, "blk", pairs)

    def across(x, odd_by, even_by):
        pairs = []
        for o in range(groups):
            for c in range(places):
                to = (o + (odd_by if c % 2 else even_by)) % groups
                pairs.append((o * places + c, to * places + c))
        return lax.ppermute(x, both, pairs)

    odd = (lax.axis_index("blk") % 2).astype(jnp.int32).reshape(1)
    scale = jnp.exp(log_scale[0])
    coef = jnp.stack([scale, scale * LOG2E, bias[0] * LOG2E])

    gate = lax.optimization_barrier
    a, b = own = normalize(odd, images, texts)
    a1 = along(a, 2, -2)
    u = along(b, -1, 1)
    b1 = along(b, -2, 2)
    state = group(odd, coef, own, ((0, 1), (1, 1)), ())
    a1, state = gate((a1, state))
    v = along(a1, -1, 1)
    a2 = along(a1, 2, -2)
    b1, u, state = gate((b1, u, state))
    b2 = along(b1, -2, 2)
    *state, ux, uy = group(
        odd, coef, own, ((1, 2), (0, 1)), (a1, u, b1), state,
        emit=((1, 0, UPPER), (1, UPPER, a.shape[0] - UPPER)),
    )
    ux, uy, v, a, b, state = gate((ux, uy, v, a, b, state))
    w2 = along(v, -2, 2)
    w1x = along(ux, 2, -2)
    w1y = along(uy, 2, -2)
    a_out = across(a, 1, -1)
    b_out = across(b, -1, 1)
    state = group(odd, coef, own, ((0, 2), (1, 1)), (v, b2, a2), state)
    state = group(odd, coef, own, ((1, 2),), (a_out, w1x), state)
    image_grad, text_grad, row_loss = group(
        odd, coef, own, ((1, 1), (0, 2)), (w1y, b_out, w2), state, (images, texts)
    )
    row_loss = row_loss.reshape(images.shape[0])
    return (row_loss, image_grad, text_grad)


def solution(mesh):
    return jax.shard_map(
        body,
        mesh=mesh,
        in_specs=(P(("outer", "blk"), None), P(("outer", "blk"), None), P(), P()),
        out_specs=(P(("outer", "blk")), P(("outer", "blk"), None), P(("outer", "blk"), None)),
        check_vma=False,
    )
```

```python
import functools

import jax
import jax.numpy as jnp
from jax import lax
from jax.experimental import pallas as pl
from jax.experimental.pallas import tpu as pltpu
from jax.sharding import PartitionSpec as P

STEPS = 4
LOG2E = 1.4426950408889634
LN2 = 0.6931471805599453
UPPER = 384
VMEM_LIMIT = 28 * 1024 * 1024
COST = 1000


def normalize_kernel(flags_ref, img_hbm, txt_hbm, a_hbm, b_hbm, near_hbm, far_hbm, raw, out, sems):
    rows = img_hbm.shape[0]
    tile = 128
    odd = flags_ref[0] == 1
    second = flags_ref[2] == 1
    loads, stores = [], []
    for k, start in enumerate(range(0, rows, tile)):
        here = pl.ds(start, tile)
        for j, ref in enumerate((img_hbm, txt_hbm)):
            loads.append(pltpu.make_async_copy(ref.at[here], raw.at[j, here], sems.at[2 * k + j]))
            loads[-1].start()
    used = len(loads)
    for k, start in enumerate(range(0, rows, tile)):
        here = pl.ds(start, tile)
        units = []
        for j in range(2):
            loads[2 * k + j].wait()
            wide = raw[j, start : start + tile, :].astype(jnp.float32)
            inverse = lax.rsqrt(jnp.sum(wide * wide, axis=-1, keepdims=True) + 1e-06)
            units.append((wide * inverse).astype(jnp.bfloat16))
        out[0, start : start + tile, :] = jnp.where(odd, units[1], units[0])
        out[1, start : start + tile, :] = jnp.where(odd, units[0], units[1])
        out[2, start : start + tile, :] = jnp.where(second, units[0], units[1])
        out[3, start : start + tile, :] = jnp.where(second, units[1], units[0])
        for role, ref in enumerate((a_hbm, b_hbm, near_hbm, far_hbm)):
            stores.append(pltpu.make_async_copy(out.at[role, here], ref.at[here], sems.at[used]))
            stores[-1].start()
            used += 1
    for store in stores:
        store.wait()


def normalize(odd, images, texts):
    rows, width = images.shape
    hbm = pl.BlockSpec(memory_space=pl.ANY)
    return pl.pallas_call(
        normalize_kernel,
        in_specs=[pl.BlockSpec(memory_space=pltpu.SMEM), hbm, hbm],
        out_specs=[hbm] * 4,
        out_shape=[jax.ShapeDtypeStruct((rows, width), jnp.bfloat16)] * 4,
        scratch_shapes=[
            pltpu.VMEM((2, rows, width), jnp.bfloat16),
            pltpu.VMEM((4, rows, width), jnp.bfloat16),
            pltpu.SemaphoreType.DMA((6 * rows // 128,)),
        ],
        compiler_params=pltpu.CompilerParams(vmem_limit_bytes=60 * 1024 * 1024),
    )(odd, images, texts)


def lane_sums(x):
    total = x[:, 0:128]
    for start in range(128, x.shape[1], 128):
        total = total + x[:, start : start + 128]
    return total


def project(raw, grad):
    wide = raw.astype(jnp.float32)
    inverse = lax.rsqrt(jnp.sum(wide * wide, axis=-1, keepdims=True) + 1e-06)
    unit = wide * inverse
    return (grad - unit * jnp.sum(unit * grad, axis=1, keepdims=True)) * inverse


def group_kernel(plan, emit, first, last, tile, odd_ref, coef_ref, *refs):
    count = sum(n for _, n in plan)
    refs = list(refs)
    take = lambda n: [refs.pop(0) for _ in range(n)]
    own = take(2)
    visits = [] if first else take(count)
    acc_in, loss_in = (None, None) if first else take(2)
    raws = take(2) if last else None
    outs = take(3 if last else 2)
    emitted = take(len(emit))
    acc, loss = take(2) if last else outs
    sems = take(1)[0] if last else None
    rows = own[0].shape[0]
    scale = coef_ref[0]
    odd = odd_ref[0] == 1
    for (k, at, n), ref in zip(emit, emitted):
        ref[...] = visits[k][at : at + n, :]
    stores = []
    done = 0
    for index, (role, n) in enumerate(plan):
        final = role not in [r for r, _ in plan[index + 1 :]]
        opening = role not in [r for r, _ in plan[:index]]
        if role >= 2:
            role = odd_ref[1] if role == 2 else 1 - odd_ref[1]
        others = [own[1 - role]] if first else visits[done : done + n]
        theirs = jnp.concatenate([ref[...] for ref in others], axis=0)
        for start in range(0, rows, tile):
            part_rows = slice(start, start + tile)
            if isinstance(role, int):
                mine = own[role][part_rows, :]
            else:
                mine = jnp.where(role == 1, own[1][part_rows, :], own[0][part_rows, :])
            dots = lax.dot_general(
                mine,
                theirs,
                (((1,), (1,)), ((), ())),
                preferred_element_type=jnp.float32,
            )
            z2 = dots * coef_ref[1] + coef_ref[2]
            e = jnp.exp2(z2)
            u = 1.0 + e
            r = 1.0 / u
            losses = jnp.log2(u) * LN2 + (e - (u - 1.0)) * r
            slope = scale * (e * r)
            if first:
                at = lax.broadcasted_iota(jnp.int32, dots.shape, 0) + start
                match = at == lax.broadcasted_iota(jnp.int32, dots.shape, 1)
                losses = jnp.where(match, losses - z2 * LN2, losses)
                slope = jnp.where(match, -scale * r, slope)
            grad = jnp.dot(slope.astype(jnp.bfloat16), theirs, preferred_element_type=jnp.float32)
            sums = lane_sums(losses)
            if not (first and opening):
                held, held_loss = (acc_in, loss_in) if opening else (acc, loss)
                grad = held[role, part_rows, :] + grad
                sums = held_loss[role, part_rows, :] + sums
            loss[role, part_rows, :] = sums
            if not (last and final):
                acc[role, part_rows, :] = grad
                continue
            is_img = odd if role == 1 else jnp.logical_not(odd)
            raw = jnp.where(is_img, raws[0][part_rows, :], raws[1][part_rows, :])
            acc[role, part_rows, :] = project(raw, grad)
            sem = sems.at[len(stores)]
            piece = acc.at[role, pl.ds(start, tile)]
            to_img = pltpu.make_async_copy(piece, outs[0].at[pl.ds(start, tile)], sem)
            to_txt = pltpu.make_async_copy(piece, outs[1].at[pl.ds(start, tile)], sem)
            pl.when(is_img)(to_img.start)
            pl.when(jnp.logical_not(is_img))(to_txt.start)
            stores.append(to_img)
        done += n
    if last:
        picked = jnp.where(odd, loss[1], loss[0])
        for k in range(rows // 128):
            block = jnp.transpose(picked[k * 128 : (k + 1) * 128, :])
            outs[2][k : k + 1, :] = jnp.sum(block, axis=0, keepdims=True) / jnp.float32((STEPS + 2) * rows)
    for store in stores:
        store.wait()


def group(odd, coef, own, plan, visits, state=None, raws=None, emit=(), tile=320):
    rows, width = own[0].shape
    first, last = state is None, raws is not None
    count = sum(n for _, n in plan)
    vmem, smem = pl.BlockSpec(memory_space=pltpu.VMEM), pl.BlockSpec(memory_space=pltpu.SMEM)
    args = [*own, *visits, *(state or ()), *(raws or ())]
    f32 = jnp.float32
    sums = [(2, rows, width), (2, rows, 128)]
    scratch = []
    if last:
        hbm = pl.BlockSpec(memory_space=pl.ANY)
        out_shape = [jax.ShapeDtypeStruct((rows, width), f32)] * 2 + [
            jax.ShapeDtypeStruct((rows // 128, 128), f32)
        ]
        out_specs = [hbm, hbm, vmem]
        scratch = [pltpu.VMEM(shape, f32) for shape in sums]
        scratch.append(pltpu.SemaphoreType.DMA((2 * rows // tile,)))
    else:
        out_shape = [jax.ShapeDtypeStruct(shape, f32) for shape in sums]
        out_shape += [jax.ShapeDtypeStruct((n, width), jnp.bfloat16) for _, _, n in emit]
        out_specs = [vmem] * len(out_shape)
    return pl.pallas_call(
        functools.partial(group_kernel, plan, emit, first, last, tile),
        in_specs=[smem, smem] + [vmem] * len(args),
        out_specs=out_specs,
        out_shape=out_shape,
        scratch_shapes=scratch,
        input_output_aliases={} if first or last else {4 + count: 0, 5 + count: 1},
        cost_estimate=pl.CostEstimate(flops=COST, bytes_accessed=COST, transcendentals=0),
        compiler_params=pltpu.CompilerParams(vmem_limit_bytes=VMEM_LIMIT),
    )(odd, coef, *args)


def body(images, texts, log_scale, bias):
    groups, places = lax.axis_size("outer"), lax.axis_size("blk")

    def along(x, odd_by, even_by):
        pairs = [(i, (i + (odd_by if i % 2 else even_by)) % places) for i in range(places)]
        return lax.ppermute(x, "blk", pairs)

    parity = lax.axis_index("blk") % 2
    second = lax.axis_index("outer") % 2
    meets = jnp.where(second == 1, parity, 1 - parity)
    odd = jnp.stack([parity, meets, second]).astype(jnp.int32)
    scale = jnp.exp(log_scale[0])
    coef = jnp.stack([scale, scale * LOG2E, bias[0] * LOG2E])

    gate = lax.optimization_barrier
    a, b, near, far = normalize(odd, images, texts)
    own = (a, b)
    a1 = along(a, 2, -2)
    u = along(b, -1, 1)
    b1 = along(b, -2, 2)
    near = lax.ppermute(near, "outer", [(o, o ^ 1) for o in range(groups)])
    state = group(odd, coef, own, ((0, 1), (1, 1)), ())
    a1, state = gate((a1, state))
    v = along(a1, -1, 1)
    a2 = along(a1, 2, -2)
    b1, u, state = gate((b1, u, state))
    b2 = along(b1, -2, 2)
    *state, ux, uy = group(
        odd, coef, own, ((1, 2), (0, 1)), (a1, u, b1), state,
        emit=((1, 0, UPPER), (1, UPPER, a.shape[0] - UPPER)),
    )
    near, state = gate((near, state))
    state = group(odd, coef, own, ((2, 1),), (near,), state)
    ux, uy, v, far, state = gate((ux, uy, v, far, state))
    w2x = along(v[:UPPER], -2, 2)
    w1x = along(ux, 2, -2)
    far = lax.ppermute(far, "outer", [(o, (o + (1 if o % 2 else -1)) % groups) for o in range(groups)])
    w2y = along(v[UPPER:], -2, 2)
    w1y = along(uy, 2, -2)
    state = group(odd, coef, own, ((0, 2), (1, 1)), (v, b2, a2), state)
    state = group(odd, coef, own, ((1, 1), (0, 1)), (w1x, w2x), state)
    state = group(odd, coef, own, ((3, 1),), (far,), state)
    image_grad, text_grad, row_loss = group(
        odd, coef, own, ((1, 1), (0, 1)), (w1y, w2y), state, (images, texts)
    )
    row_loss = row_loss.reshape(images.shape[0])
    return (row_loss, image_grad, text_grad)


def solution(mesh):
    return jax.shard_map(
        body,
        mesh=mesh,
        in_specs=(P(("outer", "blk"), None), P(("outer", "blk"), None), P(), P()),
        out_specs=(P(("outer", "blk")), P(("outer", "blk"), None), P(("outer", "blk"), None)),
        check_vma=False,
    )
```

```python
import functools

import jax
import jax.numpy as jnp
from jax import lax
from jax.experimental import pallas as pl
from jax.experimental.pallas import tpu as pltpu
from jax.sharding import PartitionSpec as P

STEPS = 4
LOG2E = 1.4426950408889634
LN2 = 0.6931471805599453
UPPER = 384
VMEM_LIMIT = 28 * 1024 * 1024
COST = 1000


def normalize_kernel(odd_ref, img_hbm, txt_hbm, a_hbm, b_hbm, raw, out, sems):
    rows = img_hbm.shape[0]
    tile = 128
    odd = odd_ref[0] == 1
    loads, stores = [], []
    for k, start in enumerate(range(0, rows, tile)):
        here = pl.ds(start, tile)
        for j, ref in enumerate((img_hbm, txt_hbm)):
            loads.append(pltpu.make_async_copy(ref.at[here], raw.at[j, here], sems.at[2 * k + j]))
            loads[-1].start()
    used = len(loads)
    for k, start in enumerate(range(0, rows, tile)):
        here = pl.ds(start, tile)
        units = []
        for j in range(2):
            loads[2 * k + j].wait()
            wide = raw[j, start : start + tile, :].astype(jnp.float32)
            inverse = lax.rsqrt(jnp.sum(wide * wide, axis=-1, keepdims=True) + 1e-06)
            units.append((wide * inverse).astype(jnp.bfloat16))
        out[0, start : start + tile, :] = jnp.where(odd, units[1], units[0])
        out[1, start : start + tile, :] = jnp.where(odd, units[0], units[1])
        for role, ref in ((0, a_hbm), (1, b_hbm)):
            stores.append(pltpu.make_async_copy(out.at[role, here], ref.at[here], sems.at[used]))
            stores[-1].start()
            used += 1
    for store in stores:
        store.wait()


def normalize(odd, images, texts):
    rows, width = images.shape
    hbm = pl.BlockSpec(memory_space=pl.ANY)
    return pl.pallas_call(
        normalize_kernel,
        in_specs=[pl.BlockSpec(memory_space=pltpu.SMEM), hbm, hbm],
        out_specs=[hbm] * 2,
        out_shape=[jax.ShapeDtypeStruct((rows, width), jnp.bfloat16)] * 2,
        scratch_shapes=[
            pltpu.VMEM((2, rows, width), jnp.bfloat16),
            pltpu.VMEM((2, rows, width), jnp.bfloat16),
            pltpu.SemaphoreType.DMA((4 * rows // 128,)),
        ],
        compiler_params=pltpu.CompilerParams(vmem_limit_bytes=60 * 1024 * 1024),
    )(odd, images, texts)


def lane_sums(x):
    total = x[:, 0:128]
    for start in range(128, x.shape[1], 128):
        total = total + x[:, start : start + 128]
    return total


def project(raw, grad):
    wide = raw.astype(jnp.float32)
    inverse = lax.rsqrt(jnp.sum(wide * wide, axis=-1, keepdims=True) + 1e-06)
    unit = wide * inverse
    return (grad - unit * jnp.sum(unit * grad, axis=1, keepdims=True)) * inverse


def group_kernel(plan, emit, first, last, tile, odd_ref, second_ref, coef_ref, *refs):
    count = sum(n for _, n in plan)
    refs = list(refs)
    take = lambda n: [refs.pop(0) for _ in range(n)]
    own = take(2)
    visits = [] if first else take(count)
    acc_in, loss_in = (None, None) if first else take(2)
    raws = take(2) if last else None
    outs = take(3 if last else 2)
    sent = take(2) if first else None
    emitted = take(len(emit))
    acc, loss = take(2) if last else outs
    sems = take(1)[0] if last else None
    rows = own[0].shape[0]
    scale = coef_ref[0]
    odd = odd_ref[0] == 1
    crossed = odd_ref[0] != second_ref[0]
    meets = jnp.where(second_ref[0] == 1, odd_ref[0], 1 - odd_ref[0])
    if first:
        sent[0][...] = jnp.where(crossed, own[0][...], own[1][...])
        sent[1][...] = jnp.where(crossed, own[1][...], own[0][...])
    for (k, at, n), ref in zip(emit, emitted):
        ref[...] = visits[k][at : at + n, :]
    stores = []
    done = 0
    for index, (role, n) in enumerate(plan):
        final = role not in [r for r, _ in plan[index + 1 :]]
        opening = role not in [r for r, _ in plan[:index]]
        if role >= 2:
            role = meets if role == 2 else 1 - meets
        others = [own[1 - role]] if first else visits[done : done + n]
        theirs = jnp.concatenate([ref[...] for ref in others], axis=0)
        for start in range(0, rows, tile):
            part_rows = slice(start, start + tile)
            if isinstance(role, int):
                mine = own[role][part_rows, :]
            else:
                mine = jnp.where(role == 1, own[1][part_rows, :], own[0][part_rows, :])
            dots = lax.dot_general(
                mine,
                theirs,
                (((1,), (1,)), ((), ())),
                preferred_element_type=jnp.float32,
            )
            z2 = dots * coef_ref[1] + coef_ref[2]
            e = jnp.exp2(z2)
            u = 1.0 + e
            r = 1.0 / u
            losses = jnp.log2(u) * LN2 + (e - (u - 1.0)) * r
            slope = scale * (e * r)
            if first:
                at = lax.broadcasted_iota(jnp.int32, dots.shape, 0) + start
                match = at == lax.broadcasted_iota(jnp.int32, dots.shape, 1)
                losses = jnp.where(match, losses - z2 * LN2, losses)
                slope = jnp.where(match, -scale * r, slope)
            grad = jnp.dot(slope.astype(jnp.bfloat16), theirs, preferred_element_type=jnp.float32)
            sums = lane_sums(losses)
            if not (first and opening):
                held, held_loss = (acc_in, loss_in) if opening else (acc, loss)
                grad = held[role, part_rows, :] + grad
                sums = held_loss[role, part_rows, :] + sums
            loss[role, part_rows, :] = sums
            if not (last and final):
                acc[role, part_rows, :] = grad
                continue
            is_img = odd if role == 1 else jnp.logical_not(odd)
            raw = jnp.where(is_img, raws[0][part_rows, :], raws[1][part_rows, :])
            acc[role, part_rows, :] = project(raw, grad)
            sem = sems.at[len(stores)]
            piece = acc.at[role, pl.ds(start, tile)]
            to_img = pltpu.make_async_copy(piece, outs[0].at[pl.ds(start, tile)], sem)
            to_txt = pltpu.make_async_copy(piece, outs[1].at[pl.ds(start, tile)], sem)
            pl.when(is_img)(to_img.start)
            pl.when(jnp.logical_not(is_img))(to_txt.start)
            stores.append(to_img)
        done += n
    if last:
        picked = jnp.where(odd, loss[1], loss[0])
        for k in range(rows // 128):
            block = jnp.transpose(picked[k * 128 : (k + 1) * 128, :])
            outs[2][k : k + 1, :] = jnp.sum(block, axis=0, keepdims=True) / jnp.float32((STEPS + 2) * rows)
    for store in stores:
        store.wait()


def group(odd, second, coef, own, plan, visits, state=None, raws=None, emit=(), tile=320):
    rows, width = own[0].shape
    first, last = state is None, raws is not None
    count = sum(n for _, n in plan)
    vmem, smem = pl.BlockSpec(memory_space=pltpu.VMEM), pl.BlockSpec(memory_space=pltpu.SMEM)
    args = [*own, *visits, *(state or ()), *(raws or ())]
    f32 = jnp.float32
    sums = [(2, rows, width), (2, rows, 128)]
    scratch = []
    if last:
        hbm = pl.BlockSpec(memory_space=pl.ANY)
        out_shape = [jax.ShapeDtypeStruct((rows, width), f32)] * 2 + [
            jax.ShapeDtypeStruct((rows // 128, 128), f32)
        ]
        out_specs = [hbm, hbm, vmem]
        scratch = [pltpu.VMEM(shape, f32) for shape in sums]
        scratch.append(pltpu.SemaphoreType.DMA((2 * rows // tile,)))
    else:
        out_shape = [jax.ShapeDtypeStruct(shape, f32) for shape in sums]
        out_shape += [jax.ShapeDtypeStruct((n, width), jnp.bfloat16) for _, _, n in emit]
        if first:
            out_shape += [jax.ShapeDtypeStruct((rows, width), jnp.bfloat16)] * 2
        out_specs = [vmem] * len(out_shape)
    return pl.pallas_call(
        functools.partial(group_kernel, plan, emit, first, last, tile),
        in_specs=[smem] * 3 + [vmem] * len(args),
        out_specs=out_specs,
        out_shape=out_shape,
        scratch_shapes=scratch,
        input_output_aliases={} if first or last else {5 + count: 0, 6 + count: 1},
        cost_estimate=pl.CostEstimate(flops=COST, bytes_accessed=COST, transcendentals=0),
        compiler_params=pltpu.CompilerParams(vmem_limit_bytes=VMEM_LIMIT),
    )(odd, second, coef, *args)


def body(images, texts, log_scale, bias):
    groups, places = lax.axis_size("outer"), lax.axis_size("blk")

    def along(x, odd_by, even_by):
        pairs = [(i, (i + (odd_by if i % 2 else even_by)) % places) for i in range(places)]
        return lax.ppermute(x, "blk", pairs)

    odd = (lax.axis_index("blk") % 2).astype(jnp.int32).reshape(1)
    second = (lax.axis_index("outer") % 2).astype(jnp.int32).reshape(1)
    scale = jnp.exp(log_scale[0])
    coef = jnp.stack([scale, scale * LOG2E, bias[0] * LOG2E])

    gate = lax.optimization_barrier
    a, b = own = normalize(odd, images, texts)
    a1 = along(a, 2, -2)
    u = along(b, -1, 1)
    b1 = along(b, -2, 2)
    *state, near, far = group(odd, second, coef, own, ((0, 1), (1, 1)), ())
    a1, state = gate((a1, state))
    v = along(a1, -1, 1)
    a2 = along(a1, 2, -2)
    b1, u, state = gate((b1, u, state))
    b2 = along(b1, -2, 2)
    near = lax.ppermute(near, "outer", [(o, o ^ 1) for o in range(groups)])
    *state, ux, uy = group(
        odd, second, coef, own, ((1, 2), (0, 1)), (a1, u, b1), state,
        emit=((1, 0, UPPER), (1, UPPER, a.shape[0] - UPPER)),
    )
    near, state = gate((near, state))
    state = group(odd, second, coef, own, ((2, 1),), (near,), state)
    ux, uy, v, far, state = gate((ux, uy, v, far, state))
    w2x = along(v[:UPPER], -2, 2)
    w1x = along(ux, 2, -2)
    far = lax.ppermute(far, "outer", [(o, (o + (1 if o % 2 else -1)) % groups) for o in range(groups)])
    w2y = along(v[UPPER:], -2, 2)
    w1y = along(uy, 2, -2)
    state = group(odd, second, coef, own, ((0, 2), (1, 1)), (v, b2, a2), state)
    state = group(odd, second, coef, own, ((1, 1), (0, 1)), (w1x, w2x), state)
    state = group(odd, second, coef, own, ((3, 1),), (far,), state)
    image_grad, text_grad, row_loss = group(
        odd, second, coef, own, ((1, 1), (0, 1)), (w1y, w2y), state, (images, texts)
    )
    row_loss = row_loss.reshape(images.shape[0])
    return (row_loss, image_grad, text_grad)


def solution(mesh):
    return jax.shard_map(
        body,
        mesh=mesh,
        in_specs=(P(("outer", "blk"), None), P(("outer", "blk"), None), P(), P()),
        out_specs=(P(("outer", "blk")), P(("outer", "blk"), None), P(("outer", "blk"), None)),
        check_vma=False,
    )
```

```python
import functools

import jax
import jax.numpy as jnp
from jax import lax
from jax.experimental import pallas as pl
from jax.experimental.pallas import tpu as pltpu
from jax.sharding import PartitionSpec as P

STEPS = 4
LOG2E = 1.4426950408889634
LN2 = 0.6931471805599453
UPPER = 384
VMEM_LIMIT = 28 * 1024 * 1024
COST = 1000


def normalize_kernel(odd_ref, img_hbm, txt_hbm, a_hbm, b_hbm, raw, out, sems):
    rows = img_hbm.shape[0]
    tile = 128
    odd = odd_ref[0] == 1
    loads, stores = [], []
    for k, start in enumerate(range(0, rows, tile)):
        here = pl.ds(start, tile)
        for j, ref in enumerate((img_hbm, txt_hbm)):
            loads.append(pltpu.make_async_copy(ref.at[here], raw.at[j, here], sems.at[2 * k + j]))
            loads[-1].start()
    used = len(loads)
    for k, start in enumerate(range(0, rows, tile)):
        here = pl.ds(start, tile)
        units = []
        for j in range(2):
            loads[2 * k + j].wait()
            wide = raw[j, start : start + tile, :].astype(jnp.float32)
            inverse = lax.rsqrt(jnp.sum(wide * wide, axis=-1, keepdims=True) + 1e-06)
            units.append((wide * inverse).astype(jnp.bfloat16))
        out[0, start : start + tile, :] = jnp.where(odd, units[1], units[0])
        out[1, start : start + tile, :] = jnp.where(odd, units[0], units[1])
        for role, ref in ((0, a_hbm), (1, b_hbm)):
            stores.append(pltpu.make_async_copy(out.at[role, here], ref.at[here], sems.at[used]))
            stores[-1].start()
            used += 1
    for store in stores:
        store.wait()


def normalize(odd, images, texts):
    rows, width = images.shape
    hbm = pl.BlockSpec(memory_space=pl.ANY)
    return pl.pallas_call(
        normalize_kernel,
        in_specs=[pl.BlockSpec(memory_space=pltpu.SMEM), hbm, hbm],
        out_specs=[hbm] * 2,
        out_shape=[jax.ShapeDtypeStruct((rows, width), jnp.bfloat16)] * 2,
        scratch_shapes=[
            pltpu.VMEM((2, rows, width), jnp.bfloat16),
            pltpu.VMEM((2, rows, width), jnp.bfloat16),
            pltpu.SemaphoreType.DMA((4 * rows // 128,)),
        ],
        compiler_params=pltpu.CompilerParams(vmem_limit_bytes=60 * 1024 * 1024),
    )(odd, images, texts)


def lane_sums(x):
    total = x[:, 0:128]
    for start in range(128, x.shape[1], 128):
        total = total + x[:, start : start + 128]
    return total


def project(raw, grad):
    wide = raw.astype(jnp.float32)
    inverse = lax.rsqrt(jnp.sum(wide * wide, axis=-1, keepdims=True) + 1e-06)
    unit = wide * inverse
    return (grad - unit * jnp.sum(unit * grad, axis=1, keepdims=True)) * inverse


def group_kernel(plan, emit, first, last, tile, odd_ref, second_ref, coef_ref, *refs):
    count = sum(n for _, n in plan)
    refs = list(refs)
    take = lambda n: [refs.pop(0) for _ in range(n)]
    own = take(2)
    visits = [] if first else take(count)
    acc_in, loss_in = (None, None) if first else take(2)
    raws = take(2) if last else None
    outs = take(3 if last else 2)
    sent = take(2) if first else None
    emitted = take(len(emit))
    acc, loss = take(2) if last else outs
    sems = take(1)[0] if last else None
    rows = own[0].shape[0]
    scale = coef_ref[0]
    odd = odd_ref[0] == 1
    crossed = odd_ref[0] != second_ref[0]
    meets = jnp.where(second_ref[0] == 1, odd_ref[0], 1 - odd_ref[0])
    if first:
        sent[0][...] = jnp.where(crossed, own[0][...], own[1][...])
        sent[1][...] = jnp.where(crossed, own[1][...], own[0][...])
    for (k, at, n), ref in zip(emit, emitted):
        ref[...] = visits[k][at : at + n, :]
    stores = []
    done = 0
    for index, (role, n) in enumerate(plan):
        final = role not in [r for r, _ in plan[index + 1 :]]
        opening = role not in [r for r, _ in plan[:index]]
        if role >= 2:
            role = meets if role == 2 else 1 - meets
        others = [own[1 - role]] if first else visits[done : done + n]
        theirs = jnp.concatenate([ref[...] for ref in others], axis=0)
        def visit_rows(start):
            part_rows = pl.ds(start, tile)
            if isinstance(role, int):
                mine = own[role][part_rows, :]
            else:
                mine = jnp.where(role == 1, own[1][part_rows, :], own[0][part_rows, :])
            dots = lax.dot_general(
                mine,
                theirs,
                (((1,), (1,)), ((), ())),
                preferred_element_type=jnp.float32,
            )
            z2 = dots * coef_ref[1] + coef_ref[2]
            e = jnp.exp2(z2)
            u = 1.0 + e
            r = 1.0 / u
            losses = jnp.log2(u) * LN2 + (e - (u - 1.0)) * r
            slope = scale * (e * r)
            if first:
                at = lax.broadcasted_iota(jnp.int32, dots.shape, 0) + start
                match = at == lax.broadcasted_iota(jnp.int32, dots.shape, 1)
                losses = jnp.where(match, losses - z2 * LN2, losses)
                slope = jnp.where(match, -scale * r, slope)
            grad = jnp.dot(slope.astype(jnp.bfloat16), theirs, preferred_element_type=jnp.float32)
            sums = lane_sums(losses)
            if not (first and opening):
                held, held_loss = (acc_in, loss_in) if opening else (acc, loss)
                grad = held[role, part_rows, :] + grad
                sums = held_loss[role, part_rows, :] + sums
            loss[role, part_rows, :] = sums
            if not (last and final):
                acc[role, part_rows, :] = grad
                return
            is_img = odd if role == 1 else jnp.logical_not(odd)
            raw = jnp.where(is_img, raws[0][part_rows, :], raws[1][part_rows, :])
            acc[role, part_rows, :] = project(raw, grad)
            sem = sems.at[len(stores)]
            piece = acc.at[role, pl.ds(start, tile)]
            to_img = pltpu.make_async_copy(piece, outs[0].at[pl.ds(start, tile)], sem)
            to_txt = pltpu.make_async_copy(piece, outs[1].at[pl.ds(start, tile)], sem)
            pl.when(is_img)(to_img.start)
            pl.when(jnp.logical_not(is_img))(to_txt.start)
            stores.append(to_img)
        if first or not isinstance(role, int):

            def turn(i, carry):
                visit_rows(pl.multiple_of(i * tile, tile))
                return carry

            lax.fori_loop(0, rows // tile, turn, 0)
        else:
            for start in range(0, rows, tile):
                visit_rows(start)
        done += n
    if last:
        picked = jnp.where(odd, loss[1], loss[0])
        for k in range(rows // 128):
            block = jnp.transpose(picked[k * 128 : (k + 1) * 128, :])
            outs[2][k : k + 1, :] = jnp.sum(block, axis=0, keepdims=True) / jnp.float32((STEPS + 2) * rows)
    for store in stores:
        store.wait()


def group(odd, second, coef, own, plan, visits, state=None, raws=None, emit=(), tile=320):
    rows, width = own[0].shape
    first, last = state is None, raws is not None
    count = sum(n for _, n in plan)
    vmem, smem = pl.BlockSpec(memory_space=pltpu.VMEM), pl.BlockSpec(memory_space=pltpu.SMEM)
    args = [*own, *visits, *(state or ()), *(raws or ())]
    f32 = jnp.float32
    sums = [(2, rows, width), (2, rows, 128)]
    scratch = []
    if last:
        hbm = pl.BlockSpec(memory_space=pl.ANY)
        out_shape = [jax.ShapeDtypeStruct((rows, width), f32)] * 2 + [
            jax.ShapeDtypeStruct((rows // 128, 128), f32)
        ]
        out_specs = [hbm, hbm, vmem]
        scratch = [pltpu.VMEM(shape, f32) for shape in sums]
        scratch.append(pltpu.SemaphoreType.DMA((2 * rows // tile,)))
    else:
        out_shape = [jax.ShapeDtypeStruct(shape, f32) for shape in sums]
        out_shape += [jax.ShapeDtypeStruct((n, width), jnp.bfloat16) for _, _, n in emit]
        if first:
            out_shape += [jax.ShapeDtypeStruct((rows, width), jnp.bfloat16)] * 2
        out_specs = [vmem] * len(out_shape)
    return pl.pallas_call(
        functools.partial(group_kernel, plan, emit, first, last, tile),
        in_specs=[smem] * 3 + [vmem] * len(args),
        out_specs=out_specs,
        out_shape=out_shape,
        scratch_shapes=scratch,
        input_output_aliases={} if first or last else {5 + count: 0, 6 + count: 1},
        cost_estimate=pl.CostEstimate(flops=COST, bytes_accessed=COST, transcendentals=0),
        compiler_params=pltpu.CompilerParams(vmem_limit_bytes=VMEM_LIMIT),
    )(odd, second, coef, *args)


def body(images, texts, log_scale, bias):
    groups, places = lax.axis_size("outer"), lax.axis_size("blk")

    def along(x, odd_by, even_by):
        pairs = [(i, (i + (odd_by if i % 2 else even_by)) % places) for i in range(places)]
        return lax.ppermute(x, "blk", pairs)

    odd = (lax.axis_index("blk") % 2).astype(jnp.int32).reshape(1)
    second = (lax.axis_index("outer") % 2).astype(jnp.int32).reshape(1)
    scale = jnp.exp(log_scale[0])
    coef = jnp.stack([scale, scale * LOG2E, bias[0] * LOG2E])

    gate = lax.optimization_barrier
    a, b = own = normalize(odd, images, texts)
    a1 = along(a, 2, -2)
    u = along(b, -1, 1)
    b1 = along(b, -2, 2)
    *state, near, far = group(odd, second, coef, own, ((0, 1), (1, 1)), ())
    a1, state = gate((a1, state))
    v = along(a1, -1, 1)
    a2 = along(a1, 2, -2)
    b1, u, state = gate((b1, u, state))
    b2 = along(b1, -2, 2)
    near = lax.ppermute(near, "outer", [(o, o ^ 1) for o in range(groups)])
    *state, ux, uy = group(
        odd, second, coef, own, ((1, 2), (0, 1)), (a1, u, b1), state,
        emit=((1, 0, UPPER), (1, UPPER, a.shape[0] - UPPER)),
    )
    near, state = gate((near, state))
    state = group(odd, second, coef, own, ((2, 1),), (near,), state)
    ux, uy, v, far, state = gate((ux, uy, v, far, state))
    w2x = along(v[:UPPER], -2, 2)
    w1x = along(ux, 2, -2)
    far = lax.ppermute(far, "outer", [(o, (o + (1 if o % 2 else -1)) % groups) for o in range(groups)])
    w2y = along(v[UPPER:], -2, 2)
    w1y = along(uy, 2, -2)
    state = group(odd, second, coef, own, ((0, 2), (1, 1)), (v, b2, a2), state)
    state = group(odd, second, coef, own, ((1, 1), (0, 1)), (w1x, w2x), state)
    state = group(odd, second, coef, own, ((3, 1),), (far,), state)
    image_grad, text_grad, row_loss = group(
        odd, second, coef, own, ((1, 1), (0, 1)), (w1y, w2y), state, (images, texts)
    )
    row_loss = row_loss.reshape(images.shape[0])
    return (row_loss, image_grad, text_grad)


def solution(mesh):
    return jax.shard_map(
        body,
        mesh=mesh,
        in_specs=(P(("outer", "blk"), None), P(("outer", "blk"), None), P(), P()),
        out_specs=(P(("outer", "blk")), P(("outer", "blk"), None), P(("outer", "blk"), None)),
        check_vma=False,
    )
```
